32 devices in a mesh: gx: 8 (over y, x, core), gy: 4 (over z).
Axes of the slice: x: 2, y: 2, z: 4, core: 2. Of those that a mesh axis runs over, the one named last changes fastest.
Arguments:
- u_vel: bfloat16 [128, 256, 1024], P(None, 'gx', 'gy'), may hold values from -6 to 6
- v_vel: bfloat16 [128, 256, 1024], P(None, 'gx', 'gy'), may hold values from -6 to 6
- inv_dx: float32 [256, 1024], P('gx', 'gy'), may hold values from 0.5 to 2
- inv_dy: float32 [256, 1024], P('gx', 'gy'), may hold values from 0.5 to 2
Outputs:
- recon_vorticity: bfloat16 [128, 256, 1024], P(None, 'gx', 'gy')
- recon_divergence: bfloat16 [128, 256, 1024], P(None, 'gx', 'gy')
The draws below stay inside these ranges and needn't reach their ends.
All inputs are finite; a program needn't handle non-finite values.
Results may differ from the reference program's by a relative error of at most 0.0045.
Values may be sent and summed in bfloat16 or wider, within the bound.
A program may use at most 64 MiB of HBM per device.

```python
import math
import jax
import jax.numpy as jnp
from jax import lax

M = 128
CX = 32
ITERS = 8
NX = 256
NY = 1024
N_GX = 8


def velocity_field(key):
    mode_count = 24
    keys = jax.random.split(key, 10)
    across = (jnp.arange(NX, dtype=jnp.float32) + 0.5) / NX
    upward = (jnp.arange(NY, dtype=jnp.float32) + 0.5) / NY
    trend = jnp.power(3.0, 0.5 * across)[:, None] * jnp.power(3.0, 0.5 * upward)[None, :]
    center_x = jax.random.uniform(keys[0], (mode_count,), jnp.float32, 0.0, 1.0)
    center_y = jax.random.uniform(keys[1], (mode_count,), jnp.float32, 0.0, 1.0)
    width_x = jax.random.uniform(keys[2], (mode_count,), jnp.float32, 0.12, 0.45)
    width_y = jax.random.uniform(keys[3], (mode_count,), jnp.float32, 0.12, 0.45)
    height = jnp.exp(jax.random.uniform(keys[4], (mode_count,), jnp.float32, math.log(0.15), math.log(0.8)))
    frequency = jnp.exp(jax.random.uniform(keys[5], (mode_count, 2), jnp.float32, math.log(0.5), math.log(24.0)))
    phase = jax.random.uniform(keys[6], (mode_count, 2), jnp.float32, -math.pi, math.pi)
    ratio = jax.random.uniform(keys[7], (mode_count,), jnp.float32, 0.0, 0.8)
    moments = jnp.arange(M, dtype=jnp.float32)
    total = jnp.zeros((M, NX, NY), jnp.float32)
    for mode in range(mode_count):
        rough = jax.random.uniform(jax.random.fold_in(keys[8], mode), (NX, NY), jnp.float32, 0.5, 1.5)
        bump_x = jnp.exp(-jnp.square((across - center_x[mode]) / width_x[mode]))
        bump_y = jnp.exp(-jnp.square((upward - center_y[mode]) / width_y[mode]))
        envelope = height[mode] * bump_x[:, None] * bump_y[None, :] * rough
        temporal = jnp.cos(2.0 * math.pi * frequency[mode, 0] * moments / M + phase[mode, 0])
        temporal = temporal + ratio[mode] * jnp.cos(2.0 * math.pi * frequency[mode, 1] * moments / M + phase[mode, 1])
        total = total + temporal[:, None, None] * envelope[None]
    signal = total * trend[None]
    noise = jnp.clip(0.3 * jax.random.normal(keys[9], (M, NX, NY), jnp.float32), -1.2, 1.2)
    return jnp.clip(signal + noise, -6.0, 6.0)


def draw_u_vel(key, part):
    return velocity_field(jax.random.fold_in(key, 11)).astype(jnp.bfloat16)


def draw_v_vel(key, part):
    return velocity_field(jax.random.fold_in(key, 23)).astype(jnp.bfloat16)


def shard_levels(rng, extent, cuts, low, top_value):
    level = 1.0
    for position, shards_of in cuts:
        steps = jax.random.uniform(jax.random.fold_in(jax.random.fold_in(rng, 6), position), (shards_of,), jnp.float32, low / len(cuts), top_value / len(cuts))
        level = level * jnp.repeat(jnp.exp(steps), extent[position] // shards_of).reshape((-1,) + (1,) * (len(extent) - 1 - position))
    return level


def setup_inputs(seed: int = 0) -> dict:
    key_of = jax.random.split(jax.random.key(seed), 5)
    return {
        "u_vel": draw_u_vel(jax.random.fold_in(key_of[4], 71), 0),
        "v_vel": draw_v_vel(jax.random.fold_in(key_of[4], 71), 0),
        "inv_dx": jnp.clip(jnp.exp(math.log(2.0) - 1.3862944 * jax.random.uniform(key_of[2], (NX, NY), jnp.float32) ** shard_levels(key_of[2], (NX, NY), ((0, 8), (1, 4)), -0.2, 0.2)), 0.5, 2.0),
        "inv_dy": jnp.clip(jnp.exp(math.log(2.0) - 1.3862944 * jax.random.uniform(key_of[3], (NX, NY), jnp.float32) ** shard_levels(key_of[3], (NX, NY), ((0, 8), (1, 4)), -0.2, 0.2)), 0.5, 2.0),
    }


def along_first(padded):
    return (padded[..., 0:-4, 2:-2] - 8.0 * padded[..., 1:-3, 2:-2] + 8.0 * padded[..., 3:-1, 2:-2] - padded[..., 4:, 2:-2]) / 12.0

def along_second(padded):
    return (padded[..., 2:-2, 0:-4] - 8.0 * padded[..., 2:-2, 1:-3] + 8.0 * padded[..., 2:-2, 3:-1] - padded[..., 2:-2, 4:]) / 12.0

def spectral_filter(gram_sum):
    order = gram_sum.shape[0]
    identity = jnp.eye(order, dtype=jnp.float32)
    shift = jnp.trace(gram_sum) / order
    scale = jnp.sqrt(jnp.sum(gram_sum * gram_sum))
    signum = (gram_sum - shift * identity) / scale
    for sweep in range(ITERS):
        square = jnp.dot(signum, signum, precision=lax.Precision.HIGHEST)
        cube = jnp.dot(signum, square, precision=lax.Precision.HIGHEST)
        signum = 1.5 * signum - 0.5 * cube
    return ((identity + signum) * 0.5).astype(jnp.bfloat16)

def reference(u_vel, v_vel, inv_dx, inv_dy):

    def snapshot_fields(pair):
        pad_u = jnp.pad(pair[0].astype(jnp.float32), 2)
        pad_v = jnp.pad(pair[1].astype(jnp.float32), 2)
        vorticity = (inv_dx * along_first(pad_v) - inv_dy * along_second(pad_u)).astype(jnp.bfloat16)
        divergence = (inv_dx * along_first(pad_u) + inv_dy * along_second(pad_v)).astype(jnp.bfloat16)
        return (vorticity, divergence)
    vorticity, divergence = lax.map(snapshot_fields, (u_vel, v_vel))
    stacked = jnp.concatenate([vorticity, divergence], 0)
    order = 2 * M

    def add_block(block_index, gram_sum):
        start = (block_index * CX).astype(jnp.int32)
        block = lax.dynamic_slice_in_dim(stacked, start, CX, 1).reshape(order, CX * NY).astype(jnp.float32)
        return gram_sum + jnp.dot(block, block.T, precision=lax.Precision.HIGHEST)
    gram_sum = lax.fori_loop(0, N_GX, add_block, jnp.zeros((order, order), jnp.float32))
    filter_bf = spectral_filter(gram_sum)
    filter_tr = filter_bf.T.astype(jnp.float32)

    def rebuild(block_index):
        start = (block_index * CX).astype(jnp.int32)
        block = lax.dynamic_slice_in_dim(stacked, start, CX, 1).reshape(order, CX * NY).astype(jnp.float32)
        mixed = jnp.dot(filter_tr, block, precision=lax.Precision.HIGHEST)
        return mixed.astype(jnp.bfloat16).reshape(order, CX, NY)
    pieces = lax.map(rebuild, jnp.arange(N_GX).astype(jnp.int32))
    rebuilt = jnp.transpose(pieces, (1, 0, 2, 3)).reshape(order, NX, NY)
    return (rebuilt[:M], rebuilt[M:])
```

```python
import functools

import jax
import jax.numpy as jnp
from jax import lax
from jax.experimental import pallas as pl
from jax.experimental.pallas import tpu as pltpu
from jax.sharding import PartitionSpec as P

ITERS = 8
EDGE = 2
SUB = 16
BATCH = 4
F32 = jnp.float32
BF16 = jnp.bfloat16
MESH = pl.DeviceIdType.MESH


def iota(shape, dim):
    return lax.broadcasted_iota(jnp.int32, shape, dim)


def swap_matrix():
    size = SUB * SUB
    row, col = iota((size, size), 0), iota((size, size), 1)
    hit = (row // SUB == col % SUB) & (row % SUB == col // SUB)
    return hit.astype(F32).astype(BF16)


def stencil_weight(gap):
    return jnp.where(
        gap == -2,
        1.0,
        jnp.where(gap == -1, -8.0, jnp.where(gap == 1, 8.0, jnp.where(gap == 2, -1.0, 0.0))),
    ).astype(BF16)


def dot(a, b):
    return jnp.dot(a, b, preferred_element_type=F32)


def dot_nt(a, b):
    return lax.dot_general(a, b, (((1,), (1,)), ((), ())), preferred_element_type=F32)


def split(x):
    high = x.astype(BF16)
    return high, (x - high.astype(F32)).astype(BF16)


def product(a, b):
    (ah, al), (bh, bl) = a, b
    return dot(
        jnp.concatenate([ah, al, ah], axis=1), jnp.concatenate([bh, bh, bl], axis=0)
    )


def spectral_filter(gram):
    order = gram.shape[0]
    eye = iota((order, order), 0) == iota((order, order), 1)

    def total(x):
        return jnp.sum(jnp.sum(x, axis=0, keepdims=True), axis=1, keepdims=True)

    shift = total(jnp.where(eye, gram, 0.0)) / order
    scale = jnp.sqrt(total(gram * gram))
    signum = (gram - jnp.where(eye, shift, 0.0)) / scale
    for sweep in range(ITERS):
        parts = split(signum)
        square = product(parts, parts)
        cube = product(parts, split(square))
        signum = 1.5 * signum - 0.5 * cube
    return ((jnp.where(eye, 1.0, 0.0) + signum) * 0.5).astype(BF16)


def pack_gram(gram, rows, count):
    half = gram.shape[0] // 2
    first, cross, second = gram[:half, :half], gram[:half, half:], gram[half:, half:]
    row, col = iota((half, half), 0), iota((half, half), 1)
    mix = jnp.where(row <= col, first, second)
    diag = jnp.sum(jnp.where(row == col, second, 0.0), axis=0, keepdims=True)
    diag = jnp.where(iota((8, half), 0) == 0, diag, 0.0)
    pad = rows * count - 2 * half - 8
    pieces = [cross, mix, diag]
    if pad:
        pieces.append(jnp.zeros((pad, half), F32))
    return jnp.concatenate(pieces, axis=0).reshape(count, rows, half)


def unpack_gram(packed):
    half = packed.shape[-1]
    flat = packed.reshape(-1, half)
    cross, mix = flat[:half], flat[half : 2 * half]
    diag = flat[2 * half : 2 * half + 1]
    row, col = iota((half, half), 0), iota((half, half), 1)
    flipped = mix.T
    first = jnp.where(row <= col, mix, flipped)
    second = jnp.where(row == col, diag, jnp.where(row > col, mix, flipped))
    top = jnp.concatenate([first, cross], axis=1)
    bottom = jnp.concatenate([cross.T, second], axis=1)
    return jnp.concatenate([top, bottom], axis=0)


def filter_kernel(
    n_gx, n_gy, snaps, tile_x, tile_y, rows,
    u_hbm, v_hbm, idx_hbm, idy_hbm,
    s_hbm, filter_ref,
    uv, inv, field, snap, strip, strip_low, strip_high, gram,
    packed, reduce_buf, z_buf, full,
    load_sem, store_sem, x_send, x_recv, y_send, y_recv,
    rs_send, rs_recv, z_send, z_recv, ag_send, ag_recv,
):
    gx, gy = lax.axis_index("gx"), lax.axis_index("gy")
    lanes = strip.shape[1]

    loads = [
        pltpu.make_async_copy(source, target, load_sem.at[i])
        for i, (source, target) in enumerate(
            [(u_hbm, uv.at[0]), (v_hbm, uv.at[1]), (idx_hbm, inv.at[0]), (idy_hbm, inv.at[1])]
        )
    ]
    for load in loads:
        load.start()

    barrier = pltpu.get_barrier_semaphore()
    for k in range(1, n_gx):
        pl.semaphore_signal(
            barrier, inc=1, device_id={"gx": lax.rem(gx + k, n_gx)}, device_id_type=MESH
        )
    for k in range(1, n_gy):
        pl.semaphore_signal(
            barrier, inc=1, device_id={"gy": lax.rem(gy + k, n_gy)}, device_id_type=MESH
        )

    def x_copy(comp, up):
        span = pl.ds(comp * snaps, snaps)
        src = field.at[pl.ds(tile_x if up else EDGE, EDGE), span]
        dst = field.at[pl.ds(0 if up else tile_x + EDGE, EDGE), span]
        return pltpu.make_async_remote_copy(
            src_ref=src, dst_ref=dst,
            send_sem=x_send.at[comp, up], recv_sem=x_recv.at[comp, up],
            device_id={"gx": gx + 1 if up else gx - 1}, device_id_type=MESH,
        )

    def y_copy(comp, up):
        span = pl.ds(comp * snaps, snaps)
        dst = strip_low if up else strip_high
        return pltpu.make_async_remote_copy(
            src_ref=strip.at[span], dst_ref=dst.at[span],
            send_sem=y_send.at[comp, up], recv_sem=y_recv.at[comp, up],
            device_id={"gy": gy + 1 if up else gy - 1}, device_id_type=MESH,
        )

    def has(index, count, up):
        return index < count - 1 if up else index > 0

    swap = swap_matrix()
    lane = iota((tile_y, lanes), 1)
    column = jnp.where(lane >= lanes // 2, tile_y - EDGE, 0) + lane % EDGE
    pick = (iota((tile_y, lanes), 0) == column).astype(F32).astype(BF16)
    group = (SUB, SUB, lanes)
    lane_x = (iota(group, 2) % (lanes // 2)) // EDGE - iota(group, 0)

    def permute(comp, j):
        first = pl.multiple_of(j * SUB, SUB)
        there = pl.multiple_of(comp * snaps + j * SUB, SUB)
        edge = jnp.zeros((SUB, lanes), F32)
        for x0 in range(0, tile_x, SUB):
            block = uv[comp, pl.ds(first, SUB), x0 : x0 + SUB, :]
            moved = dot(swap, block.reshape(SUB * SUB, tile_y)).astype(BF16)
            field[EDGE + x0 : EDGE + x0 + SUB, pl.ds(there, SUB), :] = moved.reshape(
                SUB, SUB, tile_y
            )
            taken = dot(moved, pick).reshape(group)
            edge = edge + jnp.sum(jnp.where(lane_x == x0, taken, 0.0), axis=0)
        strip[pl.ds(there, SUB), :] = edge.astype(BF16)

    for comp in range(2):
        loads[comp].wait()

        def permute_some(step, carry, comp=comp):
            for i in range(BATCH):
                permute(comp, step * BATCH + i)
            return carry

        lax.fori_loop(0, snaps // SUB // BATCH, permute_some, 0)
        if comp == 0:
            pl.semaphore_wait(barrier, n_gx + n_gy - 2)
        for up in range(2):
            @pl.when(has(gy, n_gy, up))
            def _(comp=comp, up=up):
                y_copy(comp, up).start()

            @pl.when(has(gx, n_gx, up))
            def _(comp=comp, up=up):
                x_copy(comp, up).start()

    @pl.when(gx == 0)
    def _():
        field[0:EDGE] = jnp.zeros((EDGE, 2 * snaps, tile_y), BF16)

    @pl.when(gx == n_gx - 1)
    def _():
        field[tile_x + EDGE :] = jnp.zeros((EDGE, 2 * snaps, tile_y), BF16)

    @pl.when(gy == 0)
    def _():
        strip_low[...] = jnp.zeros((2 * snaps, lanes), BF16)

    @pl.when(gy == n_gy - 1)
    def _():
        strip_high[...] = jnp.zeros((2 * snaps, lanes), BF16)

    for load in loads[2:]:
        load.wait()
    inv[...] = inv[...] * (1.0 / 12.0)
    gram[...] = jnp.zeros_like(gram)
    within = stencil_weight(iota((tile_y, tile_y), 0) - iota((tile_y, tile_y), 1))
    spot = iota((lanes, tile_y), 0)
    outer = jnp.where(spot >= lanes // 2, -EDGE, tile_y) + spot % EDGE
    beyond = stencil_weight(outer - iota((lanes, tile_y), 1))

    def wait_arrivals(copy, index, count):
        for comp in range(2):
            for up in range(2):
                @pl.when(has(index, count, 1 - up))
                def _(comp=comp, up=up):
                    copy(comp, up).wait_recv()

    wait_arrivals(y_copy, gy, n_gy)
    wide = (2 * snaps, lanes)
    halo = jnp.where(
        iota(wide, 1) >= lanes // 2, strip_low[...].astype(F32), strip_high[...].astype(F32)
    )
    strip_low[...] = halo.astype(BF16)
    owner = (iota(wide, 1) % (lanes // 2)) // EDGE

    def fields(x0, count):
        middle = field[pl.ds(x0 + EDGE, count)].reshape(count * 2 * snaps, tile_y)
        side = strip_low[...].astype(F32)
        sides = [jnp.where(owner == x0 + i, side, 0.0).astype(BF16) for i in range(count)]
        along_y = dot(middle, within) + dot(jnp.concatenate(sides, axis=0), beyond)
        done = []
        for i in range(count):
            near = field[x0 + i + 3].astype(F32) - field[x0 + i + 1].astype(F32)
            far = field[x0 + i].astype(F32) - field[x0 + i + 4].astype(F32)
            along_x = far + 8.0 * near
            at = along_y[i * 2 * snaps : (i + 1) * 2 * snaps]
            idx, idy = inv[0, pl.ds(x0 + i, 1), :], inv[1, pl.ds(x0 + i, 1), :]
            vorticity = idx * along_x[snaps:] - idy * at[:snaps]
            divergence = idx * along_x[:snaps] + idy * at[snaps:]
            both = jnp.concatenate([vorticity, divergence], axis=0).astype(BF16)
            snap[x0 + i] = both
            done.append(both)
        flat = jnp.concatenate(done, axis=1)
        gram[...] += dot_nt(flat, flat)

    def interior(step, carry):
        fields(EDGE + step * BATCH, BATCH)
        return carry

    lax.fori_loop(0, (tile_x - 2 * EDGE) // BATCH, interior, 0)
    wait_arrivals(x_copy, gx, n_gx)
    fields(0, EDGE)
    fields(tile_x - EDGE, EDGE)

    store = pltpu.make_async_copy(snap, s_hbm, store_sem)
    store.start()

    packed[...] = pack_gram(gram[...], rows, n_gx)

    def rs_copy(k):
        peer = lax.rem(gx + k, n_gx)
        return pltpu.make_async_remote_copy(
            src_ref=packed.at[peer], dst_ref=reduce_buf.at[k],
            send_sem=rs_send.at[k], recv_sem=rs_recv.at[k],
            device_id={"gx": peer}, device_id_type=MESH,
        )

    def z_copy(k):
        return pltpu.make_async_remote_copy(
            src_ref=z_buf.at[0], dst_ref=z_buf.at[k],
            send_sem=z_send.at[k], recv_sem=z_recv.at[k],
            device_id={"gy": lax.rem(gy + k, n_gy)}, device_id_type=MESH,
        )

    def ag_copy(k, block):
        return pltpu.make_async_remote_copy(
            src_ref=full.at[block], dst_ref=full.at[block],
            send_sem=ag_send.at[k], recv_sem=ag_recv.at[k],
            device_id={"gx": lax.rem(gx + k, n_gx)}, device_id_type=MESH,
        )

    for k in range(1, n_gx):
        rs_copy(k).start()
    mine = packed[gx]
    for k in range(1, n_gx):
        rs_copy(k).wait_recv()
        mine = mine + reduce_buf[k]
    z_buf[0] = mine
    for k in range(1, n_gy):
        z_copy(k).start()
    for k in range(1, n_gy):
        z_copy(k).wait_recv()
    total = z_buf[lax.rem(gy, n_gy)]
    for z in range(1, n_gy):
        total = total + z_buf[lax.rem(gy - z + n_gy, n_gy)]
    full[gx] = total
    for k in range(1, n_gx):
        ag_copy(k, gx).start()
    for k in range(1, n_gx):
        ag_copy(k, lax.rem(gx - k + n_gx, n_gx)).wait_recv()

    filter_ref[...] = spectral_filter(unpack_gram(full[...]))

    for comp in range(2):
        for up in range(2):
            @pl.when(has(gy, n_gy, up))
            def _(comp=comp, up=up):
                y_copy(comp, up).wait_send()

            @pl.when(has(gx, n_gx, up))
            def _(comp=comp, up=up):
                x_copy(comp, up).wait_send()
    for k in range(1, n_gx):
        rs_copy(k).wait_send()
        ag_copy(k, gx).wait_send()
    for k in range(1, n_gy):
        z_copy(k).wait_send()
    store.wait()


def rebuild_kernel(s_ref, filter_ref, vort_ref, div_ref, mixed):
    count, order, tile_y = s_ref.shape
    half = order // 2
    for x in range(count):
        mixed[x] = dot(filter_ref[...], s_ref[x]).astype(BF16)
    swap = swap_matrix()
    for first in range(0, order, SUB):
        block = mixed[:, first : first + SUB, :].reshape(SUB * SUB, tile_y)
        back = dot(swap, block).astype(BF16).reshape(SUB, SUB, tile_y)
        out = vort_ref if first < half else div_ref
        start = first % half
        out[start : start + SUB] = back


def per_device(n_gx, n_gy, u_vel, v_vel, inv_dx, inv_dy):
    snaps, tile_x, tile_y = u_vel.shape
    order = 2 * snaps
    lanes = 2 * EDGE * tile_x
    rows = -(-(order + 8) // (8 * n_gx)) * 8
    any_spec = pl.BlockSpec(memory_space=pl.ANY)
    dma = pltpu.SemaphoreType.DMA
    snapshots, spectral = pl.pallas_call(
        functools.partial(filter_kernel, n_gx, n_gy, snaps, tile_x, tile_y, rows),
        out_shape=(
            jax.ShapeDtypeStruct((tile_x, order, tile_y), BF16),
            jax.ShapeDtypeStruct((order, order), BF16),
        ),
        in_specs=[any_spec] * 4,
        out_specs=(any_spec, pl.BlockSpec(memory_space=pltpu.VMEM)),
        scratch_shapes=[
            pltpu.VMEM((2, snaps, tile_x, tile_y), BF16),
            pltpu.VMEM((2, tile_x, tile_y), F32),
            pltpu.VMEM((tile_x + 2 * EDGE, order, tile_y), BF16),
            pltpu.VMEM((tile_x, order, tile_y), BF16),
            pltpu.VMEM((order, lanes), BF16),
            pltpu.VMEM((order, lanes), BF16),
            pltpu.VMEM((order, lanes), BF16),
            pltpu.VMEM((order, order), F32),
            pltpu.VMEM((n_gx, rows, snaps), F32),
            pltpu.VMEM((n_gx, rows, snaps), F32),
            pltpu.VMEM((n_gy, rows, snaps), F32),
            pltpu.VMEM((n_gx, rows, snaps), F32),
            dma((4,)),
            dma,
            dma((2, 2)),
            dma((2, 2)),
            dma((2, 2)),
            dma((2, 2)),
            dma((n_gx,)),
            dma((n_gx,)),
            dma((n_gy,)),
            dma((n_gy,)),
            dma((n_gx,)),
            dma((n_gx,)),
        ],
        compiler_params=pltpu.CompilerParams(
            collective_id=0, has_side_effects=True, vmem_limit_bytes=40 * 2**20
        ),
        name="filter",
    )(u_vel, v_vel, inv_dx, inv_dy)
    out = jax.ShapeDtypeStruct((snaps, tile_x, tile_y), BF16)
    block = pl.BlockSpec((snaps, SUB, tile_y), lambda i: (0, i, 0))
    return pl.pallas_call(
        rebuild_kernel,
        out_shape=(out, out),
        grid=(tile_x // SUB,),
        in_specs=[
            pl.BlockSpec((SUB, order, tile_y), lambda i: (i, 0, 0)),
            pl.BlockSpec((order, order), lambda i: (0, 0)),
        ],
        out_specs=(block, block),
        scratch_shapes=[pltpu.VMEM((SUB, order, tile_y), BF16)],
        compiler_params=pltpu.CompilerParams(vmem_limit_bytes=40 * 2**20),
        name="rebuild",
    )(snapshots, spectral)


def solution(mesh):
    in_specs = (P(None, "gx", "gy"), P(None, "gx", "gy"), P("gx", "gy"), P("gx", "gy"))
    out_specs = (P(None, "gx", "gy"), P(None, "gx", "gy"))
    return jax.shard_map(
        functools.partial(per_device, mesh.shape["gx"], mesh.shape["gy"]),
        mesh=mesh, in_specs=in_specs, out_specs=out_specs, check_vma=False,
    )
```

```python
import functools

import jax
import jax.numpy as jnp
from jax import lax
from jax.experimental import pallas as pl
from jax.experimental.pallas import tpu as pltpu
from jax.sharding import PartitionSpec as P

ITERS = 8
EDGE = 2
SUB = 16
BATCH = 4
VMEM_BYTES = 60 * 2**20
F32 = jnp.float32
BF16 = jnp.bfloat16
MESH = pl.DeviceIdType.MESH


def iota(shape, dim):
    return lax.broadcasted_iota(jnp.int32, shape, dim)


def swap_matrix():
    size = SUB * SUB
    row, col = iota((size, size), 0), iota((size, size), 1)
    hit = (row // SUB == col % SUB) & (row % SUB == col // SUB)
    return hit.astype(F32).astype(BF16)


def stencil_weight(gap):
    return jnp.where(
        gap == -2,
        1.0,
        jnp.where(gap == -1, -8.0, jnp.where(gap == 1, 8.0, jnp.where(gap == 2, -1.0, 0.0))),
    ).astype(BF16)


def dot(a, b):
    return jnp.dot(a, b, preferred_element_type=F32)


def dot_nt(a, b):
    return lax.dot_general(a, b, (((1,), (1,)), ((), ())), preferred_element_type=F32)


def split(x):
    high = x.astype(BF16)
    return high, (x - high.astype(F32)).astype(BF16)


def product(a, b):
    (ah, al), (bh, bl) = a, b
    return dot(
        jnp.concatenate([ah, al, ah], axis=1), jnp.concatenate([bh, bh, bl], axis=0)
    )


def spectral_filter(gram):
    order = gram.shape[0]
    eye = iota((order, order), 0) == iota((order, order), 1)

    def total(x):
        return jnp.sum(jnp.sum(x, axis=0, keepdims=True), axis=1, keepdims=True)

    shift = total(jnp.where(eye, gram, 0.0)) / order
    scale = jnp.sqrt(total(gram * gram))
    signum = (gram - jnp.where(eye, shift, 0.0)) / scale
    for sweep in range(ITERS):
        parts = split(signum)
        square = product(parts, parts)
        cube = product(parts, split(square))
        signum = 1.5 * signum - 0.5 * cube
    return ((jnp.where(eye, 1.0, 0.0) + signum) * 0.5).astype(BF16)


def pack_gram(gram, rows, count):
    half = gram.shape[0] // 2
    first, cross, second = gram[:half, :half], gram[:half, half:], gram[half:, half:]
    row, col = iota((half, half), 0), iota((half, half), 1)
    mix = jnp.where(row <= col, first, second)
    diag = jnp.sum(jnp.where(row == col, second, 0.0), axis=0, keepdims=True)
    diag = jnp.where(iota((8, half), 0) == 0, diag, 0.0)
    pad = rows * count - 2 * half - 8
    pieces = [cross, mix, diag]
    if pad:
        pieces.append(jnp.zeros((pad, half), F32))
    return jnp.concatenate(pieces, axis=0).reshape(count, rows, half)


def unpack_gram(packed):
    half = packed.shape[-1]
    flat = packed.reshape(-1, half)
    cross, mix = flat[:half], flat[half : 2 * half]
    diag = flat[2 * half : 2 * half + 1]
    row, col = iota((half, half), 0), iota((half, half), 1)
    flipped = mix.T
    first = jnp.where(row <= col, mix, flipped)
    second = jnp.where(row == col, diag, jnp.where(row > col, mix, flipped))
    top = jnp.concatenate([first, cross], axis=1)
    bottom = jnp.concatenate([cross.T, second], axis=1)
    return jnp.concatenate([top, bottom], axis=0)


def filter_kernel(
    n_gx, n_gy, snaps, tile_x, tile_y, rows,
    u_hbm, v_hbm, idx_hbm, idy_hbm,
    s_hbm, filter_ref,
    uv, inv, field, partial, snap, strip, strip_low, strip_high, gram,
    packed, reduce_buf, z_buf, full,
    load_sem, store_sem, x_send, x_recv, y_send, y_recv,
    rs_send, rs_recv, z_send, z_recv, ag_send, ag_recv,
):
    gx, gy = lax.axis_index("gx"), lax.axis_index("gy")
    lanes = strip.shape[1]
    used = -(-(2 * snaps + 8) // rows)

    loads = [
        pltpu.make_async_copy(source, target, load_sem.at[i])
        for i, (source, target) in enumerate(
            [(u_hbm, uv.at[0]), (v_hbm, uv.at[1]), (idx_hbm, inv.at[0]), (idy_hbm, inv.at[1])]
        )
    ]
    for load in loads:
        load.start()

    barrier = pltpu.get_barrier_semaphore()
    for k in range(1, n_gx):
        pl.semaphore_signal(
            barrier, inc=1, device_id={"gx": lax.rem(gx + k, n_gx)}, device_id_type=MESH
        )
    for k in range(1, n_gy):
        pl.semaphore_signal(
            barrier, inc=1, device_id={"gy": lax.rem(gy + k, n_gy)}, device_id_type=MESH
        )

    def x_copy(comp, up):
        span = pl.ds(comp * snaps, snaps)
        src = field.at[pl.ds(tile_x if up else EDGE, EDGE), span]
        dst = field.at[pl.ds(0 if up else tile_x + EDGE, EDGE), span]
        return pltpu.make_async_remote_copy(
            src_ref=src, dst_ref=dst,
            send_sem=x_send.at[comp, up], recv_sem=x_recv.at[comp, up],
            device_id={"gx": gx + 1 if up else gx - 1}, device_id_type=MESH,
        )

    def y_copy(comp, up):
        span = pl.ds(comp * snaps, snaps)
        dst = strip_low if up else strip_high
        return pltpu.make_async_remote_copy(
            src_ref=strip.at[span], dst_ref=dst.at[span],
            send_sem=y_send.at[comp, up], recv_sem=y_recv.at[comp, up],
            device_id={"gy": gy + 1 if up else gy - 1}, device_id_type=MESH,
        )

    def has(index, count, up):
        return index < count - 1 if up else index > 0

    swap = swap_matrix()
    lane = iota((tile_y, lanes), 1)
    column = jnp.where(lane >= lanes // 2, tile_y - EDGE, 0) + lane % EDGE
    pick = (iota((tile_y, lanes), 0) == column).astype(F32).astype(BF16)
    group = (SUB, SUB, lanes)
    lane_x = (iota(group, 2) % (lanes // 2)) // EDGE - iota(group, 0)

    def permute(comp, j):
        first = pl.multiple_of(j * SUB, SUB)
        there = pl.multiple_of(comp * snaps + j * SUB, SUB)
        edge = jnp.zeros((SUB, lanes), F32)
        for x0 in range(0, tile_x, SUB):
            block = uv[comp, pl.ds(first, SUB), x0 : x0 + SUB, :]
            moved = dot(swap, block.reshape(SUB * SUB, tile_y)).astype(BF16)
            field[EDGE + x0 : EDGE + x0 + SUB, pl.ds(there, SUB), :] = moved.reshape(
                SUB, SUB, tile_y
            )
            taken = dot(moved, pick).reshape(group)
            edge = edge + jnp.sum(jnp.where(lane_x == x0, taken, 0.0), axis=0)
        strip[pl.ds(there, SUB), :] = edge.astype(BF16)

    for comp in range(2):
        loads[comp].wait()

        def permute_some(step, carry, comp=comp):
            for i in range(BATCH):
                permute(comp, step * BATCH + i)
            return carry

        lax.fori_loop(0, snaps // SUB // BATCH, permute_some, 0)
        if comp == 0:
            pl.semaphore_wait(barrier, n_gx + n_gy - 2)
        for up in range(2):
            @pl.when(has(gy, n_gy, up))
            def _(comp=comp, up=up):
                y_copy(comp, up).start()

            @pl.when(has(gx, n_gx, up))
            def _(comp=comp, up=up):
                x_copy(comp, up).start()

    @pl.when(gx == 0)
    def _():
        field[0:EDGE] = jnp.zeros((EDGE, 2 * snaps, tile_y), BF16)

    @pl.when(gx == n_gx - 1)
    def _():
        field[tile_x + EDGE :] = jnp.zeros((EDGE, 2 * snaps, tile_y), BF16)

    @pl.when(gy == 0)
    def _():
        strip_low[...] = jnp.zeros((2 * snaps, lanes), BF16)

    @pl.when(gy == n_gy - 1)
    def _():
        strip_high[...] = jnp.zeros((2 * snaps, lanes), BF16)

    for load in loads[2:]:
        load.wait()
    inv[...] = inv[...] * (1.0 / 12.0)
    gram[...] = jnp.zeros_like(gram)
    within = stencil_weight(iota((tile_y, tile_y), 0) - iota((tile_y, tile_y), 1))
    spot = iota((lanes, tile_y), 0)
    outer = jnp.where(spot >= lanes // 2, -EDGE, tile_y) + spot % EDGE
    beyond = stencil_weight(outer - iota((lanes, tile_y), 1))

    def inland(x0, count):
        middle = field[pl.ds(x0 + EDGE, count)].reshape(count * 2 * snaps, tile_y)
        along_y = dot(middle, within)
        for i in range(count):
            near = field[x0 + i + 3].astype(F32) - field[x0 + i + 1].astype(F32)
            far = field[x0 + i].astype(F32) - field[x0 + i + 4].astype(F32)
            along_x = far + 8.0 * near
            at = along_y[i * 2 * snaps : (i + 1) * 2 * snaps]
            idx, idy = inv[0, pl.ds(x0 + i, 1), :], inv[1, pl.ds(x0 + i, 1), :]
            partial[x0 + i, :snaps] = idx * along_x[snaps:] - idy * at[:snaps]
            partial[x0 + i, snaps:] = idx * along_x[:snaps] + idy * at[snaps:]

    def interior(step, carry):
        inland(EDGE + step * BATCH, BATCH)
        return carry

    lax.fori_loop(0, (tile_x - 2 * EDGE) // BATCH, interior, 0)

    def wait_arrivals(copy, index, count):
        for comp in range(2):
            for up in range(2):
                @pl.when(has(index, count, 1 - up))
                def _(comp=comp, up=up):
                    copy(comp, up).wait_recv()

    wait_arrivals(x_copy, gx, n_gx)
    inland(0, EDGE)
    inland(tile_x - EDGE, EDGE)
    wait_arrivals(y_copy, gy, n_gy)
    wide = (2 * snaps, lanes)
    halo = jnp.where(
        iota(wide, 1) >= lanes // 2, strip_low[...].astype(F32), strip_high[...].astype(F32)
    )
    halo = jnp.where(iota(wide, 0) < snaps, -halo, halo)
    strip_low[...] = halo.astype(BF16)
    owner = (iota(wide, 1) % (lanes // 2)) // EDGE

    def finish(step, carry):
        x0 = step * BATCH
        side = strip_low[...].astype(F32)
        sides = [jnp.where(owner == x0 + i, side, 0.0).astype(BF16) for i in range(BATCH)]
        rest = dot(jnp.concatenate(sides, axis=0), beyond)
        done = []
        for i in range(BATCH):
            idy = inv[1, pl.ds(x0 + i, 1), :]
            both = partial[x0 + i] + idy * rest[i * 2 * snaps : (i + 1) * 2 * snaps]
            both = both.astype(BF16)
            snap[x0 + i] = both
            done.append(both)
        flat = jnp.concatenate(done, axis=1)
        gram[...] += dot_nt(flat, flat)
        return carry

    lax.fori_loop(0, tile_x // BATCH, finish, 0)

    store = pltpu.make_async_copy(snap, s_hbm, store_sem)
    store.start()

    packed[...] = pack_gram(gram[...], rows, n_gx)

    def rs_copy(k):
        peer = lax.rem(gx + k, n_gx)
        return pltpu.make_async_remote_copy(
            src_ref=packed.at[peer], dst_ref=reduce_buf.at[k],
            send_sem=rs_send.at[k], recv_sem=rs_recv.at[k],
            device_id={"gx": peer}, device_id_type=MESH,
        )

    def z_copy(k):
        return pltpu.make_async_remote_copy(
            src_ref=z_buf.at[0], dst_ref=z_buf.at[k],
            send_sem=z_send.at[k], recv_sem=z_recv.at[k],
            device_id={"gy": lax.rem(gy + k, n_gy)}, device_id_type=MESH,
        )

    def ag_copy(k, block):
        return pltpu.make_async_remote_copy(
            src_ref=full.at[block], dst_ref=full.at[block],
            send_sem=ag_send.at[k], recv_sem=ag_recv.at[k],
            device_id={"gx": lax.rem(gx + k, n_gx)}, device_id_type=MESH,
        )

    def owns(peer):
        return peer < used

    for k in range(1, n_gx):
        @pl.when(owns(lax.rem(gx + k, n_gx)))
        def _(k=k):
            rs_copy(k).start()

    @pl.when(owns(gx))
    def _():
        mine = packed[gx]
        for k in range(1, n_gx):
            rs_copy(k).wait_recv()
            mine = mine + reduce_buf[k]
        z_buf[0] = mine
        for k in range(1, n_gy):
            z_copy(k).start()
        for k in range(1, n_gy):
            z_copy(k).wait_recv()
        total = z_buf[gy]
        for z in range(1, n_gy):
            total = total + z_buf[lax.rem(gy - z + n_gy, n_gy)]
        full[gx] = total
        for k in range(1, n_gx):
            ag_copy(k, gx).start()

    for k in range(1, n_gx):
        sender = lax.rem(gx - k + n_gx, n_gx)

        @pl.when(owns(sender))
        def _(k=k, sender=sender):
            ag_copy(k, sender).wait_recv()

    filter_ref[...] = spectral_filter(unpack_gram(full[...]))

    for comp in range(2):
        for up in range(2):
            @pl.when(has(gy, n_gy, up))
            def _(comp=comp, up=up):
                y_copy(comp, up).wait_send()

            @pl.when(has(gx, n_gx, up))
            def _(comp=comp, up=up):
                x_copy(comp, up).wait_send()
    for k in range(1, n_gx):
        @pl.when(owns(lax.rem(gx + k, n_gx)))
        def _(k=k):
            rs_copy(k).wait_send()

    @pl.when(owns(gx))
    def _():
        for k in range(1, n_gx):
            ag_copy(k, gx).wait_send()
        for k in range(1, n_gy):
            z_copy(k).wait_send()

    store.wait()


def rebuild_kernel(
    s_hbm, filter_hbm, vort_hbm, div_hbm, snap, filter_ref, mixed, out, filter_sem, in_sem, out_sem
):
    tile_x, order, tile_y = snap.shape
    half = order // 2
    part = SUB // 2
    filter_load = pltpu.make_async_copy(filter_hbm, filter_ref, filter_sem)
    filter_load.start()
    loads = []
    for i in range(tile_x // part):
        span = pl.ds(i * part, part)
        loads.append(pltpu.make_async_copy(s_hbm.at[span], snap.at[span], in_sem.at[i]))
        loads[-1].start()
    swap = swap_matrix()
    filter_load.wait()
    stores = []
    for x0 in range(0, tile_x, SUB):
        for x in range(x0, x0 + SUB):
            if x % part == 0:
                loads[x // part].wait()
            mixed[x] = dot(filter_ref[...], snap[x]).astype(BF16)
        for first in range(0, order, SUB):
            block = mixed[x0 : x0 + SUB, first : first + SUB, :]
            back = dot(swap, block.reshape(SUB * SUB, tile_y)).astype(BF16)
            field, start = first // half, first % half
            where = (pl.ds(start, SUB), pl.ds(x0, SUB))
            out[field, start : start + SUB, x0 : x0 + SUB, :] = back.reshape(SUB, SUB, tile_y)
            store = pltpu.make_async_copy(
                out.at[field].at[where],
                (vort_hbm, div_hbm)[field].at[where],
                out_sem.at[x0 // SUB, first // SUB],
            )
            store.start()
            stores.append(store)
    for store in stores:
        store.wait()


def per_device(n_gx, n_gy, u_vel, v_vel, inv_dx, inv_dy):
    snaps, tile_x, tile_y = u_vel.shape
    order = 2 * snaps
    lanes = 2 * EDGE * tile_x
    rows = -(-(order + 8) // (8 * n_gx)) * 8
    any_spec = pl.BlockSpec(memory_space=pl.ANY)
    dma = pltpu.SemaphoreType.DMA
    snapshots, spectral = pl.pallas_call(
        functools.partial(filter_kernel, n_gx, n_gy, snaps, tile_x, tile_y, rows),
        out_shape=(
            jax.ShapeDtypeStruct((tile_x, order, tile_y), BF16),
            jax.ShapeDtypeStruct((order, order), BF16),
        ),
        in_specs=[any_spec] * 4,
        out_specs=(any_spec, pl.BlockSpec(memory_space=pltpu.VMEM)),
        scratch_shapes=[
            pltpu.VMEM((2, snaps, tile_x, tile_y), BF16),
            pltpu.VMEM((2, tile_x, tile_y), F32),
            pltpu.VMEM((tile_x + 2 * EDGE, order, tile_y), BF16),
            pltpu.VMEM((tile_x, order, tile_y), F32),
            pltpu.VMEM((tile_x, order, tile_y), BF16),
            pltpu.VMEM((order, lanes), BF16),
            pltpu.VMEM((order, lanes), BF16),
            pltpu.VMEM((order, lanes), BF16),
            pltpu.VMEM((order, order), F32),
            pltpu.VMEM((n_gx, rows, snaps), F32),
            pltpu.VMEM((n_gx, rows, snaps), F32),
            pltpu.VMEM((n_gy, rows, snaps), F32),
            pltpu.VMEM((n_gx, rows, snaps), F32),
            dma((4,)),
            dma,
            dma((2, 2)),
            dma((2, 2)),
            dma((2, 2)),
            dma((2, 2)),
            dma((n_gx,)),
            dma((n_gx,)),
            dma((n_gy,)),
            dma((n_gy,)),
            dma((n_gx,)),
            dma((n_gx,)),
        ],
        compiler_params=pltpu.CompilerParams(
            collective_id=0, has_side_effects=True, vmem_limit_bytes=VMEM_BYTES
        ),
        name="filter",
    )(u_vel, v_vel, inv_dx, inv_dy)
    out = jax.ShapeDtypeStruct((snaps, tile_x, tile_y), BF16)
    return pl.pallas_call(
        rebuild_kernel,
        out_shape=(out, out),
        in_specs=[any_spec, any_spec],
        out_specs=(any_spec, any_spec),
        scratch_shapes=[
            pltpu.VMEM((tile_x, order, tile_y), BF16),
            pltpu.VMEM((order, order), BF16),
            pltpu.VMEM((tile_x, order, tile_y), BF16),
            pltpu.VMEM((2, snaps, tile_x, tile_y), BF16),
            dma,
            dma((2 * tile_x // SUB,)),
            dma((tile_x // SUB, order // SUB)),
        ],
        compiler_params=pltpu.CompilerParams(vmem_limit_bytes=VMEM_BYTES),
        name="rebuild",
    )(snapshots, spectral)


def solution(mesh):
    in_specs = (P(None, "gx", "gy"), P(None, "gx", "gy"), P("gx", "gy"), P("gx", "gy"))
    out_specs = (P(None, "gx", "gy"), P(None, "gx", "gy"))
    return jax.shard_map(
        functools.partial(per_device, mesh.shape["gx"], mesh.shape["gy"]),
        mesh=mesh, in_specs=in_specs, out_specs=out_specs, check_vma=False,
    )
```

```python
import functools

import jax
import jax.numpy as jnp
from jax import lax
from jax.experimental import pallas as pl
from jax.experimental.pallas import tpu as pltpu
from jax.sharding import PartitionSpec as P

ITERS = 8
EDGE = 2
SUB = 16
BATCH = 4
VMEM_BYTES = 60 * 2**20
F32 = jnp.float32
BF16 = jnp.bfloat16
MESH = pl.DeviceIdType.MESH


def iota(shape, dim):
    return lax.broadcasted_iota(jnp.int32, shape, dim)


def swap_matrix():
    size = SUB * SUB
    row, col = iota((size, size), 0), iota((size, size), 1)
    hit = (row // SUB == col % SUB) & (row % SUB == col // SUB)
    return hit.astype(F32).astype(BF16)


def stencil_weight(gap):
    return jnp.where(
        gap == -2,
        1.0,
        jnp.where(gap == -1, -8.0, jnp.where(gap == 1, 8.0, jnp.where(gap == 2, -1.0, 0.0))),
    ).astype(BF16)


def dot(a, b):
    return jnp.dot(a, b, preferred_element_type=F32)


def dot_nt(a, b):
    return lax.dot_general(a, b, (((1,), (1,)), ((), ())), preferred_element_type=F32)


def split(x):
    high = x.astype(BF16)
    return high, (x - high.astype(F32)).astype(BF16)


def product(a, b):
    (ah, al), (bh, bl) = a, b
    return dot(
        jnp.concatenate([ah, al, ah], axis=1), jnp.concatenate([bh, bh, bl], axis=0)
    )


def spectral_filter(gram):
    order = gram.shape[0]
    eye = iota((order, order), 0) == iota((order, order), 1)

    def total(x):
        return jnp.sum(jnp.sum(x, axis=0, keepdims=True), axis=1, keepdims=True)

    shift = total(jnp.where(eye, gram, 0.0)) / order
    scale = jnp.sqrt(total(gram * gram))
    signum = (gram - jnp.where(eye, shift, 0.0)) / scale
    for sweep in range(ITERS):
        parts = split(signum)
        square = product(parts, parts)
        cube = product(parts, split(square))
        signum = 1.5 * signum - 0.5 * cube
    return ((jnp.where(eye, 1.0, 0.0) + signum) * 0.5).astype(BF16)


def pack_gram(gram, rows, count):
    half = gram.shape[0] // 2
    first, cross, second = gram[:half, :half], gram[:half, half:], gram[half:, half:]
    row, col = iota((half, half), 0), iota((half, half), 1)
    mix = jnp.where(row <= col, first, second)
    diag = jnp.sum(jnp.where(row == col, second, 0.0), axis=0, keepdims=True)
    diag = jnp.where(iota((8, half), 0) == 0, diag, 0.0)
    pad = rows * count - 2 * half - 8
    pieces = [cross, mix, diag]
    if pad:
        pieces.append(jnp.zeros((pad, half), F32))
    return jnp.concatenate(pieces, axis=0).reshape(count, rows, half)


def unpack_gram(packed):
    half = packed.shape[-1]
    flat = packed.reshape(-1, half)
    cross, mix = flat[:half], flat[half : 2 * half]
    diag = flat[2 * half : 2 * half + 1]
    row, col = iota((half, half), 0), iota((half, half), 1)
    flipped = mix.T
    first = jnp.where(row <= col, mix, flipped)
    second = jnp.where(row == col, diag, jnp.where(row > col, mix, flipped))
    top = jnp.concatenate([first, cross], axis=1)
    bottom = jnp.concatenate([cross.T, second], axis=1)
    return jnp.concatenate([top, bottom], axis=0)


def filter_kernel(
    n_gx, n_gy, snaps, tile_x, tile_y, rows,
    u_hbm, v_hbm, idx_hbm, idy_hbm,
    s_hbm, filter_ref,
    uv, inv, field, partial, snap, strip, strip_low, strip_high, gram,
    packed, reduce_buf, z_buf, full,
    load_sem, store_sem, x_send, x_recv, y_send, y_recv,
    rs_send, rs_recv, z_send, z_recv, ag_send, ag_recv,
):
    gx, gy = lax.axis_index("gx"), lax.axis_index("gy")
    lanes = strip.shape[1]
    used = -(-(2 * snaps + 8) // rows)

    span = SUB * BATCH
    loads = []
    for comp, source in enumerate((u_hbm, v_hbm)):
        for first in range(0, snaps, span):
            at = pl.ds(first, span)
            loads.append((source.at[at], uv.at[comp, at]))
    loads += [(idx_hbm, inv.at[0]), (idy_hbm, inv.at[1])]
    loads = [pltpu.make_async_copy(*pair, load_sem.at[i]) for i, pair in enumerate(loads)]
    for load in loads:
        load.start()

    barrier = pltpu.get_barrier_semaphore()
    for k in range(1, n_gx):
        pl.semaphore_signal(
            barrier, inc=1, device_id={"gx": lax.rem(gx + k, n_gx)}, device_id_type=MESH
        )
    for k in range(1, n_gy):
        pl.semaphore_signal(
            barrier, inc=1, device_id={"gy": lax.rem(gy + k, n_gy)}, device_id_type=MESH
        )

    def x_copy(comp, up):
        span = pl.ds(comp * snaps, snaps)
        src = field.at[pl.ds(tile_x if up else EDGE, EDGE), span]
        dst = field.at[pl.ds(0 if up else tile_x + EDGE, EDGE), span]
        return pltpu.make_async_remote_copy(
            src_ref=src, dst_ref=dst,
            send_sem=x_send.at[comp, up], recv_sem=x_recv.at[comp, up],
            device_id={"gx": gx + 1 if up else gx - 1}, device_id_type=MESH,
        )

    def y_copy(comp, up):
        span = pl.ds(comp * snaps, snaps)
        dst = strip_low if up else strip_high
        return pltpu.make_async_remote_copy(
            src_ref=strip.at[span], dst_ref=dst.at[span],
            send_sem=y_send.at[comp, up], recv_sem=y_recv.at[comp, up],
            device_id={"gy": gy + 1 if up else gy - 1}, device_id_type=MESH,
        )

    def has(index, count, up):
        return index < count - 1 if up else index > 0

    swap = swap_matrix()
    lane = iota((tile_y, lanes), 1)
    column = jnp.where(lane >= lanes // 2, tile_y - EDGE, 0) + lane % EDGE
    pick = (iota((tile_y, lanes), 0) == column).astype(F32).astype(BF16)
    group = (SUB, SUB, lanes)
    lane_x = (iota(group, 2) % (lanes // 2)) // EDGE - iota(group, 0)

    def permute(comp, j):
        first, there = j * SUB, comp * snaps + j * SUB
        edge = jnp.zeros((SUB, lanes), F32)
        for x0 in range(0, tile_x, SUB):
            block = uv[comp, pl.ds(first, SUB), x0 : x0 + SUB, :]
            moved = dot(swap, block.reshape(SUB * SUB, tile_y)).astype(BF16)
            field[EDGE + x0 : EDGE + x0 + SUB, pl.ds(there, SUB), :] = moved.reshape(
                SUB, SUB, tile_y
            )
            taken = dot(moved, pick).reshape(group)
            edge = edge + jnp.sum(jnp.where(lane_x == x0, taken, 0.0), axis=0)
        strip[pl.ds(there, SUB), :] = edge.astype(BF16)

    for comp in range(2):
        steps = snaps // span
        for step in range(steps):
            loads[comp * steps + step].wait()
            for i in range(BATCH):
                permute(comp, step * BATCH + i)
        if comp == 0:
            pl.semaphore_wait(barrier, n_gx + n_gy - 2)
        for up in range(2):
            @pl.when(has(gy, n_gy, up))
            def _(comp=comp, up=up):
                y_copy(comp, up).start()

            @pl.when(has(gx, n_gx, up))
            def _(comp=comp, up=up):
                x_copy(comp, up).start()

    @pl.when(gx == 0)
    def _():
        field[0:EDGE] = jnp.zeros((EDGE, 2 * snaps, tile_y), BF16)

    @pl.when(gx == n_gx - 1)
    def _():
        field[tile_x + EDGE :] = jnp.zeros((EDGE, 2 * snaps, tile_y), BF16)

    @pl.when(gy == 0)
    def _():
        strip_low[...] = jnp.zeros((2 * snaps, lanes), BF16)

    @pl.when(gy == n_gy - 1)
    def _():
        strip_high[...] = jnp.zeros((2 * snaps, lanes), BF16)

    for load in loads[-2:]:
        load.wait()
    inv[...] = inv[...] * (1.0 / 12.0)
    gram[...] = jnp.zeros_like(gram)
    within = stencil_weight(iota((tile_y, tile_y), 0) - iota((tile_y, tile_y), 1))
    spot = iota((lanes, tile_y), 0)
    outer = jnp.where(spot >= lanes // 2, -EDGE, tile_y) + spot % EDGE
    beyond = stencil_weight(outer - iota((lanes, tile_y), 1))

    def inland(x0, count):
        middle = field[pl.ds(x0 + EDGE, count)].reshape(count * 2 * snaps, tile_y)
        along_y = dot(middle, within)
        for i in range(count):
            near = field[x0 + i + 3].astype(F32) - field[x0 + i + 1].astype(F32)
            far = field[x0 + i].astype(F32) - field[x0 + i + 4].astype(F32)
            along_x = far + 8.0 * near
            at = along_y[i * 2 * snaps : (i + 1) * 2 * snaps]
            idx, idy = inv[0, pl.ds(x0 + i, 1), :], inv[1, pl.ds(x0 + i, 1), :]
            partial[x0 + i, :snaps] = idx * along_x[snaps:] - idy * at[:snaps]
            partial[x0 + i, snaps:] = idx * along_x[:snaps] + idy * at[snaps:]

    def interior(step, carry):
        inland(EDGE + step * BATCH, BATCH)
        return carry

    lax.fori_loop(0, (tile_x - 2 * EDGE) // BATCH, interior, 0)

    def wait_arrivals(copy, index, count):
        for comp in range(2):
            for up in range(2):
                @pl.when(has(index, count, 1 - up))
                def _(comp=comp, up=up):
                    copy(comp, up).wait_recv()

    wait_arrivals(x_copy, gx, n_gx)
    inland(0, EDGE)
    inland(tile_x - EDGE, EDGE)
    wait_arrivals(y_copy, gy, n_gy)
    wide = (2 * snaps, lanes)
    halo = jnp.where(
        iota(wide, 1) >= lanes // 2, strip_low[...].astype(F32), strip_high[...].astype(F32)
    )
    halo = jnp.where(iota(wide, 0) < snaps, -halo, halo)
    strip_low[...] = halo.astype(BF16)
    owner = (iota(wide, 1) % (lanes // 2)) // EDGE

    def finish(step, carry):
        x0 = step * BATCH
        side = strip_low[...].astype(F32)
        sides = [jnp.where(owner == x0 + i, side, 0.0).astype(BF16) for i in range(BATCH)]
        rest = dot(jnp.concatenate(sides, axis=0), beyond)
        done = []
        for i in range(BATCH):
            idy = inv[1, pl.ds(x0 + i, 1), :]
            both = partial[x0 + i] + idy * rest[i * 2 * snaps : (i + 1) * 2 * snaps]
            both = both.astype(BF16)
            snap[x0 + i] = both
            done.append(both)
        flat = jnp.concatenate(done, axis=1)
        gram[...] += dot_nt(flat, flat)
        return carry

    lax.fori_loop(0, tile_x // BATCH, finish, 0)

    store = pltpu.make_async_copy(snap, s_hbm, store_sem)
    store.start()

    packed[...] = pack_gram(gram[...], rows, n_gx)

    cut = -(-rows // 16) * 8
    spans = [pl.ds(0, cut), pl.ds(cut, rows - cut)] if cut < rows else [pl.ds(0, rows)]
    pieces = range(len(spans))

    def rs_copy(p, k):
        peer = lax.rem(gx + k, n_gx)
        return pltpu.make_async_remote_copy(
            src_ref=packed.at[peer, spans[p]], dst_ref=reduce_buf.at[k, spans[p]],
            send_sem=rs_send.at[p, k], recv_sem=rs_recv.at[p, k],
            device_id={"gx": peer}, device_id_type=MESH,
        )

    def z_copy(p, k):
        return pltpu.make_async_remote_copy(
            src_ref=z_buf.at[0, spans[p]], dst_ref=z_buf.at[k, spans[p]],
            send_sem=z_send.at[p, k], recv_sem=z_recv.at[p, k],
            device_id={"gy": lax.rem(gy + k, n_gy)}, device_id_type=MESH,
        )

    def ag_copy(p, k, block):
        return pltpu.make_async_remote_copy(
            src_ref=full.at[block, spans[p]], dst_ref=full.at[block, spans[p]],
            send_sem=ag_send.at[p, k], recv_sem=ag_recv.at[p, k],
            device_id={"gx": lax.rem(gx + k, n_gx)}, device_id_type=MESH,
        )

    def owns(peer):
        return peer < used

    for p in pieces:
        for k in range(1, n_gx):
            @pl.when(owns(lax.rem(gx + k, n_gx)))
            def _(p=p, k=k):
                rs_copy(p, k).start()

    @pl.when(owns(gx))
    def _():
        for p in pieces:
            mine = packed[gx, spans[p]]
            for k in range(1, n_gx):
                rs_copy(p, k).wait_recv()
                mine = mine + reduce_buf[k, spans[p]]
            z_buf[0, spans[p]] = mine
            for k in range(1, n_gy):
                z_copy(p, k).start()
        for p in pieces:
            for k in range(1, n_gy):
                z_copy(p, k).wait_recv()
            total = z_buf[gy, spans[p]]
            for z in range(1, n_gy):
                total = total + z_buf[lax.rem(gy - z + n_gy, n_gy), spans[p]]
            full[gx, spans[p]] = total
            for k in range(1, n_gx):
                ag_copy(p, k, gx).start()

    for p in pieces:
        for k in range(1, n_gx):
            sender = lax.rem(gx - k + n_gx, n_gx)

            @pl.when(owns(sender))
            def _(p=p, k=k, sender=sender):
                ag_copy(p, k, sender).wait_recv()

    filter_ref[...] = spectral_filter(unpack_gram(full[...]))

    for comp in range(2):
        for up in range(2):
            @pl.when(has(gy, n_gy, up))
            def _(comp=comp, up=up):
                y_copy(comp, up).wait_send()

            @pl.when(has(gx, n_gx, up))
            def _(comp=comp, up=up):
                x_copy(comp, up).wait_send()
    for p in pieces:
        for k in range(1, n_gx):
            @pl.when(owns(lax.rem(gx + k, n_gx)))
            def _(p=p, k=k):
                rs_copy(p, k).wait_send()

    @pl.when(owns(gx))
    def _():
        for p in pieces:
            for k in range(1, n_gx):
                ag_copy(p, k, gx).wait_send()
            for k in range(1, n_gy):
                z_copy(p, k).wait_send()

    store.wait()


def rebuild_kernel(
    s_hbm, filter_hbm, vort_hbm, div_hbm, snap, filter_ref, mixed, out, filter_sem, in_sem, out_sem
):
    tile_x, order, tile_y = snap.shape
    half = order // 2
    part = SUB // 2
    filter_load = pltpu.make_async_copy(filter_hbm, filter_ref, filter_sem)
    filter_load.start()
    loads = []
    for i in range(tile_x // part):
        span = pl.ds(i * part, part)
        loads.append(pltpu.make_async_copy(s_hbm.at[span], snap.at[span], in_sem.at[i]))
        loads[-1].start()
    swap = swap_matrix()
    filter_load.wait()
    stores = []
    for x0 in range(0, tile_x, SUB):
        for x in range(x0, x0 + SUB):
            if x % part == 0:
                loads[x // part].wait()
            mixed[x] = dot(filter_ref[...], snap[x]).astype(BF16)
        for first in range(0, order, SUB):
            block = mixed[x0 : x0 + SUB, first : first + SUB, :]
            back = dot(swap, block.reshape(SUB * SUB, tile_y)).astype(BF16)
            field, start = first // half, first % half
            out[field, start : start + SUB, x0 : x0 + SUB, :] = back.reshape(SUB, SUB, tile_y)
            if start + SUB == half:
                span = pl.ds(x0, SUB)
                store = pltpu.make_async_copy(
                    out.at[field, :, span],
                    (vort_hbm, div_hbm)[field].at[:, span],
                    out_sem.at[x0 // SUB, field],
                )
                store.start()
                stores.append(store)
    for store in stores:
        store.wait()


def per_device(n_gx, n_gy, u_vel, v_vel, inv_dx, inv_dy):
    snaps, tile_x, tile_y = u_vel.shape
    order = 2 * snaps
    lanes = 2 * EDGE * tile_x
    rows = -(-(order + 8) // (8 * n_gx)) * 8
    any_spec = pl.BlockSpec(memory_space=pl.ANY)
    dma = pltpu.SemaphoreType.DMA
    snapshots, spectral = pl.pallas_call(
        functools.partial(filter_kernel, n_gx, n_gy, snaps, tile_x, tile_y, rows),
        out_shape=(
            jax.ShapeDtypeStruct((tile_x, order, tile_y), BF16),
            jax.ShapeDtypeStruct((order, order), BF16),
        ),
        in_specs=[any_spec] * 4,
        out_specs=(any_spec, pl.BlockSpec(memory_space=pltpu.VMEM)),
        scratch_shapes=[
            pltpu.VMEM((2, snaps, tile_x, tile_y), BF16),
            pltpu.VMEM((2, tile_x, tile_y), F32),
            pltpu.VMEM((tile_x + 2 * EDGE, order, tile_y), BF16),
            pltpu.VMEM((tile_x, order, tile_y), F32),
            pltpu.VMEM((tile_x, order, tile_y), BF16),
            pltpu.VMEM((order, lanes), BF16),
            pltpu.VMEM((order, lanes), BF16),
            pltpu.VMEM((order, lanes), BF16),
            pltpu.VMEM((order, order), F32),
            pltpu.VMEM((n_gx, rows, snaps), F32),
            pltpu.VMEM((n_gx, rows, snaps), F32),
            pltpu.VMEM((n_gy, rows, snaps), F32),
            pltpu.VMEM((n_gx, rows, snaps), F32),
            dma((2 * snaps // (SUB * BATCH) + 2,)),
            dma,
            dma((2, 2)),
            dma((2, 2)),
            dma((2, 2)),
            dma((2, 2)),
            dma((2, n_gx)),
            dma((2, n_gx)),
            dma((2, n_gy)),
            dma((2, n_gy)),
            dma((2, n_gx)),
            dma((2, n_gx)),
        ],
        compiler_params=pltpu.CompilerParams(
            collective_id=0, has_side_effects=True, vmem_limit_bytes=VMEM_BYTES
        ),
        name="filter",
    )(u_vel, v_vel, inv_dx, inv_dy)
    out = jax.ShapeDtypeStruct((snaps, tile_x, tile_y), BF16)
    return pl.pallas_call(
        rebuild_kernel,
        out_shape=(out, out),
        in_specs=[any_spec, any_spec],
        out_specs=(any_spec, any_spec),
        scratch_shapes=[
            pltpu.VMEM((tile_x, order, tile_y), BF16),
            pltpu.VMEM((order, order), BF16),
            pltpu.VMEM((tile_x, order, tile_y), BF16),
            pltpu.VMEM((2, snaps, tile_x, tile_y), BF16),
            dma,
            dma((2 * tile_x // SUB,)),
            dma((tile_x // SUB, 2)),
        ],
        compiler_params=pltpu.CompilerParams(vmem_limit_bytes=VMEM_BYTES),
        name="rebuild",
    )(snapshots, spectral)


def solution(mesh):
    in_specs = (P(None, "gx", "gy"), P(None, "gx", "gy"), P("gx", "gy"), P("gx", "gy"))
    out_specs = (P(None, "gx", "gy"), P(None, "gx", "gy"))
    return jax.shard_map(
        functools.partial(per_device, mesh.shape["gx"], mesh.shape["gy"]),
        mesh=mesh, in_specs=in_specs, out_specs=out_specs, check_vma=False,
    )
```

```python
import functools

import jax
import jax.numpy as jnp
from jax import lax
from jax.experimental import pallas as pl
from jax.experimental.pallas import tpu as pltpu
from jax.sharding import PartitionSpec as P

ITERS = 8
EDGE = 2
SUB = 16
BATCH = 4
PARTS = 4
VMEM_BYTES = 48 * 2**20
F32 = jnp.float32
BF16 = jnp.bfloat16
MESH = pl.DeviceIdType.MESH


def iota(shape, dim):
    return lax.broadcasted_iota(jnp.int32, shape, dim)


def swap_matrix():
    size = SUB * SUB
    row, col = iota((size, size), 0), iota((size, size), 1)
    hit = (row // SUB == col % SUB) & (row % SUB == col // SUB)
    return hit.astype(F32).astype(BF16)


def stencil_weight(gap):
    return jnp.where(
        gap == -2,
        1.0,
        jnp.where(gap == -1, -8.0, jnp.where(gap == 1, 8.0, jnp.where(gap == 2, -1.0, 0.0))),
    ).astype(BF16)


def dot(a, b):
    return jnp.dot(a, b, preferred_element_type=F32)


def dot_nt(a, b):
    return lax.dot_general(a, b, (((1,), (1,)), ((), ())), preferred_element_type=F32)


def split(x):
    high = x.astype(BF16)
    return high, (x - high.astype(F32)).astype(BF16)


def product(a, b):
    (ah, al), (bh, bl) = a, b
    return dot(
        jnp.concatenate([ah, al, ah], axis=1), jnp.concatenate([bh, bh, bl], axis=0)
    )


def spectral_filter(gram):
    order = gram.shape[0]
    eye = iota((order, order), 0) == iota((order, order), 1)

    def total(x):
        return jnp.sum(jnp.sum(x, axis=0, keepdims=True), axis=1, keepdims=True)

    shift = total(jnp.where(eye, gram, 0.0)) / order
    scale = jnp.sqrt(total(gram * gram))
    signum = (gram - jnp.where(eye, shift, 0.0)) / scale
    for sweep in range(ITERS):
        parts = split(signum)
        square = product(parts, parts)
        cube = product(parts, split(square))
        signum = 1.5 * signum - 0.5 * cube
    return ((jnp.where(eye, 1.0, 0.0) + signum) * 0.5).astype(BF16)


def pack_gram(gram, rows, count):
    half = gram.shape[0] // 2
    first, cross, second = gram[:half, :half], gram[:half, half:], gram[half:, half:]
    row, col = iota((half, half), 0), iota((half, half), 1)
    mix = jnp.where(row <= col, first, second)
    diag = jnp.sum(jnp.where(row == col, second, 0.0), axis=0, keepdims=True)
    diag = jnp.where(iota((8, half), 0) == 0, diag, 0.0)
    pad = rows * count - 2 * half - 8
    pieces = [cross, mix, diag]
    if pad:
        pieces.append(jnp.zeros((pad, half), F32))
    return jnp.concatenate(pieces, axis=0).reshape(count, rows, half)


def unpack_gram(packed):
    half = packed.shape[-1]
    flat = packed.reshape(-1, half)
    cross, mix = flat[:half], flat[half : 2 * half]
    diag = flat[2 * half : 2 * half + 1]
    row, col = iota((half, half), 0), iota((half, half), 1)
    flipped = mix.T
    first = jnp.where(row <= col, mix, flipped)
    second = jnp.where(row == col, diag, jnp.where(row > col, mix, flipped))
    top = jnp.concatenate([first, cross], axis=1)
    bottom = jnp.concatenate([cross.T, second], axis=1)
    return jnp.concatenate([top, bottom], axis=0)


def filter_kernel(
    n_gx, n_gy, snaps, tile_x, tile_y, rows,
    u_hbm, v_hbm, idx_hbm, idy_hbm,
    s_parts, filter_ref,
    uv, inv, field, partial, snap, strip, strip_low, strip_high, gram,
    packed, reduce_buf, z_buf, full,
    load_sem, store_sem, x_send, x_recv, y_send, y_recv,
    rs_send, rs_recv, z_send, z_recv, ag_send, ag_recv,
):
    gx, gy = lax.axis_index("gx"), lax.axis_index("gy")
    lanes = strip.shape[1]
    used = -(-(2 * snaps + 8) // rows)

    span = SUB * BATCH
    loads = []
    for comp, source in enumerate((u_hbm, v_hbm)):
        for first in range(0, snaps, span):
            at = pl.ds(first, span)
            loads.append((source.at[at], uv.at[comp, at]))
    loads += [(idx_hbm, inv.at[0]), (idy_hbm, inv.at[1])]
    loads = [pltpu.make_async_copy(*pair, load_sem.at[i]) for i, pair in enumerate(loads)]
    for load in loads:
        load.start()

    barrier = pltpu.get_barrier_semaphore()
    for k in range(1, n_gx):
        pl.semaphore_signal(
            barrier, inc=1, device_id={"gx": lax.rem(gx + k, n_gx)}, device_id_type=MESH
        )
    for k in range(1, n_gy):
        pl.semaphore_signal(
            barrier, inc=1, device_id={"gy": lax.rem(gy + k, n_gy)}, device_id_type=MESH
        )

    def x_copy(comp, up):
        span = pl.ds(comp * snaps, snaps)
        src = field.at[pl.ds(tile_x if up else EDGE, EDGE), span]
        dst = field.at[pl.ds(0 if up else tile_x + EDGE, EDGE), span]
        return pltpu.make_async_remote_copy(
            src_ref=src, dst_ref=dst,
            send_sem=x_send.at[comp, up], recv_sem=x_recv.at[comp, up],
            device_id={"gx": gx + 1 if up else gx - 1}, device_id_type=MESH,
        )

    def y_copy(comp, up):
        span = pl.ds(comp * snaps, snaps)
        dst = strip_low if up else strip_high
        return pltpu.make_async_remote_copy(
            src_ref=strip.at[span], dst_ref=dst.at[span],
            send_sem=y_send.at[comp, up], recv_sem=y_recv.at[comp, up],
            device_id={"gy": gy + 1 if up else gy - 1}, device_id_type=MESH,
        )

    def has(index, count, up):
        return index < count - 1 if up else index > 0

    swap = swap_matrix()
    lane = iota((tile_y, lanes), 1)
    column = jnp.where(lane >= lanes // 2, tile_y - EDGE, 0) + lane % EDGE
    pick = (iota((tile_y, lanes), 0) == column).astype(F32).astype(BF16)
    group = (SUB, SUB, lanes)
    lane_x = (iota(group, 2) % (lanes // 2)) // EDGE - iota(group, 0)

    def permute(comp, j):
        first, there = j * SUB, comp * snaps + j * SUB
        edge = jnp.zeros((SUB, lanes), F32)
        for x0 in range(0, tile_x, SUB):
            block = uv[comp, pl.ds(first, SUB), x0 : x0 + SUB, :]
            moved = dot(swap, block.reshape(SUB * SUB, tile_y)).astype(BF16)
            field[EDGE + x0 : EDGE + x0 + SUB, pl.ds(there, SUB), :] = moved.reshape(
                SUB, SUB, tile_y
            )
            taken = dot(moved, pick).reshape(group)
            edge = edge + jnp.sum(jnp.where(lane_x == x0, taken, 0.0), axis=0)
        strip[pl.ds(there, SUB), :] = edge.astype(BF16)

    for comp in range(2):
        steps = snaps // span
        for step in range(steps):
            loads[comp * steps + step].wait()
            for i in range(BATCH):
                permute(comp, step * BATCH + i)
        if comp == 0:
            pl.semaphore_wait(barrier, n_gx + n_gy - 2)
        for up in range(2):
            @pl.when(has(gy, n_gy, up))
            def _(comp=comp, up=up):
                y_copy(comp, up).start()

            @pl.when(has(gx, n_gx, up))
            def _(comp=comp, up=up):
                x_copy(comp, up).start()

    @pl.when(gx == 0)
    def _():
        field[0:EDGE] = jnp.zeros((EDGE, 2 * snaps, tile_y), BF16)

    @pl.when(gx == n_gx - 1)
    def _():
        field[tile_x + EDGE :] = jnp.zeros((EDGE, 2 * snaps, tile_y), BF16)

    @pl.when(gy == 0)
    def _():
        strip_low[...] = jnp.zeros((2 * snaps, lanes), BF16)

    @pl.when(gy == n_gy - 1)
    def _():
        strip_high[...] = jnp.zeros((2 * snaps, lanes), BF16)

    for load in loads[-2:]:
        load.wait()
    inv[...] = inv[...] * (1.0 / 12.0)
    gram[...] = jnp.zeros_like(gram)
    within = stencil_weight(iota((tile_y, tile_y), 0) - iota((tile_y, tile_y), 1))
    spot = iota((lanes, tile_y), 0)
    outer = jnp.where(spot >= lanes // 2, -EDGE, tile_y) + spot % EDGE
    beyond = stencil_weight(outer - iota((lanes, tile_y), 1))

    def inland(x0, count):
        middle = field[pl.ds(x0 + EDGE, count)].reshape(count * 2 * snaps, tile_y)
        along_y = dot(middle, within)
        for i in range(count):
            near = field[x0 + i + 3].astype(F32) - field[x0 + i + 1].astype(F32)
            far = field[x0 + i].astype(F32) - field[x0 + i + 4].astype(F32)
            along_x = far + 8.0 * near
            at = along_y[i * 2 * snaps : (i + 1) * 2 * snaps]
            idx, idy = inv[0, pl.ds(x0 + i, 1), :], inv[1, pl.ds(x0 + i, 1), :]
            partial[x0 + i, :snaps] = idx * along_x[snaps:] - idy * at[:snaps]
            partial[x0 + i, snaps:] = idx * along_x[:snaps] + idy * at[snaps:]

    def interior(step, carry):
        inland(EDGE + step * BATCH, BATCH)
        return carry

    lax.fori_loop(0, (tile_x - 2 * EDGE) // BATCH, interior, 0)

    def wait_arrivals(copy, index, count):
        for comp in range(2):
            for up in range(2):
                @pl.when(has(index, count, 1 - up))
                def _(comp=comp, up=up):
                    copy(comp, up).wait_recv()

    wait_arrivals(x_copy, gx, n_gx)
    inland(0, EDGE)
    inland(tile_x - EDGE, EDGE)
    wait_arrivals(y_copy, gy, n_gy)
    wide = (2 * snaps, lanes)
    halo = jnp.where(
        iota(wide, 1) >= lanes // 2, strip_low[...].astype(F32), strip_high[...].astype(F32)
    )
    halo = jnp.where(iota(wide, 0) < snaps, -halo, halo)
    strip_low[...] = halo.astype(BF16)
    owner = (iota(wide, 1) % (lanes // 2)) // EDGE

    def finish(step, carry):
        x0 = step * BATCH
        side = strip_low[...].astype(F32)
        sides = [jnp.where(owner == x0 + i, side, 0.0).astype(BF16) for i in range(BATCH)]
        rest = dot(jnp.concatenate(sides, axis=0), beyond)
        done = []
        for i in range(BATCH):
            idy = inv[1, pl.ds(x0 + i, 1), :]
            both = partial[x0 + i] + idy * rest[i * 2 * snaps : (i + 1) * 2 * snaps]
            both = both.astype(BF16)
            snap[x0 + i] = both
            done.append(both)
        flat = jnp.concatenate(done, axis=1)
        gram[...] += dot_nt(flat, flat)
        return carry

    lax.fori_loop(0, tile_x // BATCH, finish, 0)

    part = tile_x // len(s_parts)
    stores = [
        pltpu.make_async_copy(snap.at[pl.ds(i * part, part)], s_part, store_sem.at[i])
        for i, s_part in enumerate(s_parts)
    ]
    for store in stores:
        store.start()

    packed[...] = pack_gram(gram[...], rows, n_gx)

    cut = -(-rows // 16) * 8
    spans = [pl.ds(0, cut), pl.ds(cut, rows - cut)] if cut < rows else [pl.ds(0, rows)]
    pieces = range(len(spans))

    def rs_copy(p, k):
        peer = lax.rem(gx + k, n_gx)
        return pltpu.make_async_remote_copy(
            src_ref=packed.at[peer, spans[p]], dst_ref=reduce_buf.at[k, spans[p]],
            send_sem=rs_send.at[p, k], recv_sem=rs_recv.at[p, k],
            device_id={"gx": peer}, device_id_type=MESH,
        )

    def z_copy(p, k):
        return pltpu.make_async_remote_copy(
            src_ref=z_buf.at[0, spans[p]], dst_ref=z_buf.at[k, spans[p]],
            send_sem=z_send.at[p, k], recv_sem=z_recv.at[p, k],
            device_id={"gy": lax.rem(gy + k, n_gy)}, device_id_type=MESH,
        )

    def ag_copy(p, k, block):
        return pltpu.make_async_remote_copy(
            src_ref=full.at[block, spans[p]], dst_ref=full.at[block, spans[p]],
            send_sem=ag_send.at[p, k], recv_sem=ag_recv.at[p, k],
            device_id={"gx": lax.rem(gx + k, n_gx)}, device_id_type=MESH,
        )

    def owns(peer):
        return peer < used

    for p in pieces:
        for k in range(1, n_gx):
            @pl.when(owns(lax.rem(gx + k, n_gx)))
            def _(p=p, k=k):
                rs_copy(p, k).start()

    @pl.when(owns(gx))
    def _():
        for p in pieces:
            mine = packed[gx, spans[p]]
            for k in range(1, n_gx):
                rs_copy(p, k).wait_recv()
                mine = mine + reduce_buf[k, spans[p]]
            z_buf[0, spans[p]] = mine
            for k in range(1, n_gy):
                z_copy(p, k).start()
        for p in pieces:
            for k in range(1, n_gy):
                z_copy(p, k).wait_recv()
            total = z_buf[gy, spans[p]]
            for z in range(1, n_gy):
                total = total + z_buf[lax.rem(gy - z + n_gy, n_gy), spans[p]]
            full[gx, spans[p]] = total
            for k in range(1, n_gx):
                ag_copy(p, k, gx).start()

    for p in pieces:
        for k in range(1, n_gx):
            sender = lax.rem(gx - k + n_gx, n_gx)

            @pl.when(owns(sender))
            def _(p=p, k=k, sender=sender):
                ag_copy(p, k, sender).wait_recv()

    filter_ref[...] = spectral_filter(unpack_gram(full[...]))

    for comp in range(2):
        for up in range(2):
            @pl.when(has(gy, n_gy, up))
            def _(comp=comp, up=up):
                y_copy(comp, up).wait_send()

            @pl.when(has(gx, n_gx, up))
            def _(comp=comp, up=up):
                x_copy(comp, up).wait_send()
    for p in pieces:
        for k in range(1, n_gx):
            @pl.when(owns(lax.rem(gx + k, n_gx)))
            def _(p=p, k=k):
                rs_copy(p, k).wait_send()

    @pl.when(owns(gx))
    def _():
        for p in pieces:
            for k in range(1, n_gx):
                ag_copy(p, k, gx).wait_send()
            for k in range(1, n_gy):
                z_copy(p, k).wait_send()

    for store in stores:
        store.wait()


def rebuild_kernel(
    s_parts, filter_ref, vort_hbm, div_hbm, mixed, out, out_sem
):
    tile_x, order, tile_y = mixed.shape
    part = tile_x // len(s_parts)
    half = order // 2
    swap = swap_matrix()
    stores = []
    for x0 in range(0, tile_x, SUB):
        for x in range(x0, x0 + SUB):
            mixed[x] = dot(filter_ref[...], s_parts[x // part][x % part]).astype(BF16)
        for first in range(0, order, SUB):
            block = mixed[x0 : x0 + SUB, first : first + SUB, :]
            back = dot(swap, block.reshape(SUB * SUB, tile_y)).astype(BF16)
            field, start = first // half, first % half
            out[field, start : start + SUB, x0 : x0 + SUB, :] = back.reshape(SUB, SUB, tile_y)
            if start + SUB == half:
                span = pl.ds(x0, SUB)
                store = pltpu.make_async_copy(
                    out.at[field, :, span],
                    (vort_hbm, div_hbm)[field].at[:, span],
                    out_sem.at[x0 // SUB, field],
                )
                store.start()
                stores.append(store)
    for store in stores:
        store.wait()


def per_device(n_gx, n_gy, u_vel, v_vel, inv_dx, inv_dy):
    snaps, tile_x, tile_y = u_vel.shape
    order = 2 * snaps
    lanes = 2 * EDGE * tile_x
    rows = -(-(order + 8) // (8 * n_gx)) * 8
    any_spec = pl.BlockSpec(memory_space=pl.ANY)
    dma = pltpu.SemaphoreType.DMA
    snapshots, spectral = pl.pallas_call(
        functools.partial(filter_kernel, n_gx, n_gy, snaps, tile_x, tile_y, rows),
        out_shape=(
            [jax.ShapeDtypeStruct((tile_x // PARTS, order, tile_y), BF16)] * PARTS,
            jax.ShapeDtypeStruct((order, order), BF16),
        ),
        in_specs=[any_spec] * 4,
        out_specs=([any_spec] * PARTS, pl.BlockSpec(memory_space=pltpu.VMEM)),
        scratch_shapes=[
            pltpu.VMEM((2, snaps, tile_x, tile_y), BF16),
            pltpu.VMEM((2, tile_x, tile_y), F32),
            pltpu.VMEM((tile_x + 2 * EDGE, order, tile_y), BF16),
            pltpu.VMEM((tile_x, order, tile_y), F32),
            pltpu.VMEM((tile_x, order, tile_y), BF16),
            pltpu.VMEM((order, lanes), BF16),
            pltpu.VMEM((order, lanes), BF16),
            pltpu.VMEM((order, lanes), BF16),
            pltpu.VMEM((order, order), F32),
            pltpu.VMEM((n_gx, rows, snaps), F32),
            pltpu.VMEM((n_gx, rows, snaps), F32),
            pltpu.VMEM((n_gy, rows, snaps), F32),
            pltpu.VMEM((n_gx, rows, snaps), F32),
            dma((2 * snaps // (SUB * BATCH) + 2,)),
            dma((PARTS,)),
            dma((2, 2)),
            dma((2, 2)),
            dma((2, 2)),
            dma((2, 2)),
            dma((2, n_gx)),
            dma((2, n_gx)),
            dma((2, n_gy)),
            dma((2, n_gy)),
            dma((2, n_gx)),
            dma((2, n_gx)),
        ],
        compiler_params=pltpu.CompilerParams(
            collective_id=0, has_side_effects=True, vmem_limit_bytes=VMEM_BYTES
        ),
        name="filter",
    )(u_vel, v_vel, inv_dx, inv_dy)
    out = jax.ShapeDtypeStruct((snaps, tile_x, tile_y), BF16)
    return pl.pallas_call(
        rebuild_kernel,
        out_shape=(out, out),
        in_specs=[[pl.BlockSpec(memory_space=pltpu.VMEM)] * PARTS, pl.BlockSpec(memory_space=pltpu.VMEM)],
        out_specs=(any_spec, any_spec),
        scratch_shapes=[
            pltpu.VMEM((tile_x, order, tile_y), BF16),
            pltpu.VMEM((2, snaps, tile_x, tile_y), BF16),
            dma((tile_x // SUB, 2)),
        ],
        compiler_params=pltpu.CompilerParams(vmem_limit_bytes=30 * 2**20),
        name="rebuild",
    )(snapshots, spectral)


def solution(mesh):
    in_specs = (P(None, "gx", "gy"), P(None, "gx", "gy"), P("gx", "gy"), P("gx", "gy"))
    out_specs = (P(None, "gx", "gy"), P(None, "gx", "gy"))
    return jax.shard_map(
        functools.partial(per_device, mesh.shape["gx"], mesh.shape["gy"]),
        mesh=mesh, in_specs=in_specs, out_specs=out_specs, check_vma=False,
    )
```
